32 devices in a mesh: grp: 2 (over x), space: 16 (over z, y, core).
Axes of the slice: x: 2, y: 2, z: 4, core: 2. Of those that a mesh axis runs over, the one named last changes fastest.
Arguments:
- inputs: bfloat16 [96, 128, 128, 128], P('grp', 'space'), parts along dimension 0, may hold values from -6 to 6
- cotangent: bfloat16 [96, 128, 128, 128], P('grp', 'space'), parts along dimension 0, may hold values from -6 to 6
- spectral_weight: bfloat16 [256, 16, 2, 2304], P('space'), may hold values from -20 to 20
- pointwise_weight: bfloat16 [48, 48], replicated, may hold values from -0.875 to 0.875
- bias: float32 [48], replicated, may hold values from -3 to 3
Outputs:
- grad_input: bfloat16 [96, 128, 128, 128], P('grp', 'space'), parts along dimension 0
- grad_spectral: float32 [512, 16, 2, 2304], P(('grp', 'space')), parts along dimension 0
- grad_pointwise: float32 [96, 48], P('grp'), parts along dimension 0
- grad_bias: float32 [96], P('grp'), parts along dimension 0
The draws below stay inside these ranges and needn't reach their ends.
There are 2 independent parts, one for each index of `grp`. The reference program is written for one: setup_inputs(seed, part) draws one part's arguments, and reference() takes and returns one part's arrays. A program takes and returns all parts, laid end to end along the dimension named above; an argument that names none is the same for every part. Nothing has to cross between parts.
All inputs are finite; a program needn't handle non-finite values.
Results may differ from the reference program's by a relative error of at most 0.0075.
Values sent between devices are 32-bit elements; how exact they have to be, the bound alone decides.
A program may use at most 192 MiB of HBM per device.

```python
import math
import jax
import jax.numpy as jnp
from jax import lax

N = 128
C = 48
M = 16


def block_levels(key, dims, pieces, least, high):
    def one(dim, blocks):
        heights = jax.random.uniform(jax.random.fold_in(jax.random.fold_in(key, 6), dim), (blocks,), jnp.float32, least / len(pieces), high / len(pieces))
        return jnp.repeat(jnp.exp(heights), dims[dim] // blocks).reshape((-1,) + (1,) * (len(dims) - dim - 1))

    factor_of = one(*pieces[0])
    for cut in pieces[1:]:
        factor_of = factor_of * one(*cut)
    return factor_of


def centred(own_key, dims, width, limit, pieces=(), held_as=jnp.bfloat16):
    entries = jax.random.normal(own_key, dims, jnp.float32) * width
    if len(pieces) > 0:
        entries = block_levels(own_key, dims, pieces, -0.22, 0.18) * entries
    return jnp.clip(entries, min=-limit, max=limit).astype(held_as)


def setup_inputs(seed: int = 0, part: int = 0) -> dict:
    streams_of = jax.random.split(jax.random.key(seed), 6)
    part_keys = jax.random.split(jax.random.fold_in(streams_of[5], part), 6)
    inputs = centred(part_keys[0], (C, N, N, N), 1.0, 6.0, ((1, 16),))
    cotangent = centred(part_keys[1], (C, N, N, N), 1.0, 6.0, ((1, 16),))
    spectral_weight = centred(streams_of[2], (M * M, M, 2, C * C), ((N // M) ** 1.5 / C ** 0.5), 20.0, ((0, 16),))
    pointwise_weight = centred(streams_of[3], (C, C), C ** -0.5, 0.875)
    bias = centred(streams_of[4], (C,), 0.5, 3.0, (), jnp.float32)
    return {"inputs": inputs, "cotangent": cotangent, "spectral_weight": spectral_weight, "pointwise_weight": pointwise_weight, "bias": bias}


HIGH = lax.Precision.HIGHEST

def phases(positions, freqs, length):
    product = positions[:, None] * freqs[None, :] % length
    angle = product.astype(jnp.float32) * (2.0 * math.pi / length)
    return (jnp.cos(angle), jnp.sin(angle))

def x_forward(real_part, imag_part, cosine, sine):
    ur = jnp.einsum('cxp,xm->pmc', real_part, cosine, precision=HIGH) + jnp.einsum('cxp,xm->pmc', imag_part, sine, precision=HIGH)
    ui = jnp.einsum('cxp,xm->pmc', imag_part, cosine, precision=HIGH) - jnp.einsum('cxp,xm->pmc', real_part, sine, precision=HIGH)
    return jnp.stack([ur, ui], 2)

def x_inverse(modes, cosine, sine):
    wr = modes[:, :, 0]
    wi = modes[:, :, 1]
    qr = jnp.einsum('pmc,xm->cxp', wr, cosine, precision=HIGH) - jnp.einsum('pmc,xm->cxp', wi, sine, precision=HIGH)
    qi = jnp.einsum('pmc,xm->cxp', wr, sine, precision=HIGH) + jnp.einsum('pmc,xm->cxp', wi, cosine, precision=HIGH)
    return jnp.stack([qr, qi], 1)

def yz_forward(section, cosine, sine):
    real_part = section[:, :M]
    imag_part = section[:, M:]
    y_real = jnp.einsum('ckxy,yj->cxjk', real_part, cosine, precision=HIGH) + jnp.einsum('ckxy,yj->cxjk', imag_part, sine, precision=HIGH)
    y_imag = jnp.einsum('ckxy,yj->cxjk', imag_part, cosine, precision=HIGH) - jnp.einsum('ckxy,yj->cxjk', real_part, sine, precision=HIGH)
    channels, planes = (y_real.shape[0], y_real.shape[1])
    return (y_real.reshape(channels, planes, M * M), y_imag.reshape(channels, planes, M * M))

def yz_inverse(stacked, cosine, sine):
    channels, planes = (stacked.shape[0], stacked.shape[2])
    qr = stacked[:, 0].reshape(channels, planes, M, M)
    qi = stacked[:, 1].reshape(channels, planes, M, M)
    rr = jnp.einsum('cxjk,yj->cxyk', qr, cosine, precision=HIGH) - jnp.einsum('cxjk,yj->cxyk', qi, sine, precision=HIGH)
    ri = jnp.einsum('cxjk,yj->cxyk', qr, sine, precision=HIGH) + jnp.einsum('cxjk,yj->cxyk', qi, cosine, precision=HIGH)
    table = jnp.concatenate([cosine.T, -sine.T], 0)
    return jnp.einsum('cxyk,kz->cxyz', jnp.concatenate([rr, ri], 3), table, precision=HIGH)

def forward_modes(field, cosine, sine):
    z_table = jnp.concatenate([cosine, -sine], 1).astype(jnp.bfloat16)
    z_table = lax.optimization_barrier(z_table).astype(jnp.float32)
    section = jnp.einsum('cxyz,zk->ckxy', field.astype(jnp.float32), z_table, precision=HIGH)
    y_real, y_imag = yz_forward(section, cosine, sine)
    return x_forward(y_real, y_imag, cosine, sine) * float(N) ** (-1.5)

def inverse_modes(modes, cosine, sine):
    return yz_inverse(x_inverse(modes, cosine, sine), cosine, sine) * float(N) ** (-1.5)

def split_weight(weight):
    pencils = weight.shape[0]
    wr = weight[:, :, 0].astype(jnp.float32).reshape(pencils, M, C, C)
    wi = weight[:, :, 1].astype(jnp.float32).reshape(pencils, M, C, C)
    return (wr, wi)

def activate(values):
    return jax.nn.gelu(values, approximate=True)

def reference(inputs, cotangent, spectral_weight, pointwise_weight, bias):
    positions = jnp.arange(N, dtype=jnp.int32)
    cosine, sine = phases(positions, jnp.arange(M, dtype=jnp.int32), N)
    inputs_hat = forward_modes(inputs, cosine, sine)
    wr, wi = split_weight(spectral_weight)
    ur, ui = (inputs_hat[:, :, 0], inputs_hat[:, :, 1])
    mr = jnp.einsum('pmi,pmio->pmo', ur, wr, precision=HIGH) - jnp.einsum('pmi,pmio->pmo', ui, wi, precision=HIGH)
    mi = jnp.einsum('pmi,pmio->pmo', ur, wi, precision=HIGH) + jnp.einsum('pmi,pmio->pmo', ui, wr, precision=HIGH)
    spectral = inverse_modes(jnp.stack([mr, mi], 2), cosine, sine)
    point = pointwise_weight.astype(jnp.float32)
    linear = jnp.einsum('oi,ixyz->oxyz', point, inputs.astype(jnp.float32), precision=HIGH)
    pre = spectral + linear + bias[:, None, None, None]
    primal, pull = jax.vjp(activate, pre)
    slope = pull(cotangent.astype(jnp.float32))[0].astype(jnp.bfloat16)
    scale = float(N) ** (-1.5)
    slope32 = slope.astype(jnp.float32)
    grad_pointwise = jnp.einsum('oxyz,ixyz->oi', slope32, inputs.astype(jnp.float32), precision=HIGH) * scale
    grad_bias = lax.optimization_barrier(jnp.sum(slope32, axis=(1, 2, 3))) * scale
    slope_hat = forward_modes(slope, cosine, sine)
    sr, si = (slope_hat[:, :, 0], slope_hat[:, :, 1])
    grad_real = jnp.einsum('pmi,pmo->pmio', ur, sr, precision=HIGH) + jnp.einsum('pmi,pmo->pmio', ui, si, precision=HIGH)
    grad_imag = jnp.einsum('pmi,pmo->pmio', ur, si, precision=HIGH) - jnp.einsum('pmi,pmo->pmio', ui, sr, precision=HIGH)
    pencils = grad_real.shape[0]
    grad_spectral = jnp.stack([grad_real, grad_imag], 2).reshape(pencils, M, 2, C * C)
    back_real = jnp.einsum('pmio,pmo->pmi', wr, sr, precision=HIGH) + jnp.einsum('pmio,pmo->pmi', wi, si, precision=HIGH)
    back_imag = jnp.einsum('pmio,pmo->pmi', wr, si, precision=HIGH) - jnp.einsum('pmio,pmo->pmi', wi, sr, precision=HIGH)
    back_field = inverse_modes(jnp.stack([back_real, back_imag], 2), cosine, sine)
    transpose_term = jnp.einsum('oi,oxyz->ixyz', point, slope32, precision=HIGH)
    grad_input = (back_field + transpose_term).astype(jnp.bfloat16)
    return (grad_input, grad_spectral, grad_pointwise, grad_bias)
```

```python
import functools
import math

import jax
import jax.numpy as jnp
import numpy as np
from jax import lax
from jax.experimental import pallas as pl
from jax.experimental.pallas import tpu as pltpu
from jax.sharding import PartitionSpec as P

M = 16
T16 = 16
HIGH = lax.Precision.HIGHEST
BF = jnp.bfloat16
F32 = jnp.float32
LIMIT = 56 * 1024 * 1024


class Plan:
    def __init__(self, space, channels, width):
        self.S = space
        self.C = channels
        self.N = width
        self.X = width // space
        self.h = space // M
        self.kl = M // self.h
        self.g = 4 * self.h
        self.G = channels // self.g
        self.L = 128 * self.h
        self.rows = self.X * self.G
        self.rp = -(-channels // space)
        self.rows_p = self.rows + 8
        self.pairs = channels * channels
        self.tables()

    def tables(self):
        S, C, N, h, kl, g, G, L = self.S, self.C, self.N, self.h, self.kl, self.g, self.G, self.L
        ang = 2.0 * np.pi * ((np.arange(N)[:, None] * np.arange(M)[None, :]) % N) / N
        cos, sin = np.cos(ang), np.sin(ang)
        scale = float(N) ** -1.5
        bf = lambda a: np.asarray(a, np.float32).astype(jnp.bfloat16)
        f32 = lambda a: np.asarray(a, np.float32)
        fwd = np.zeros((g, N, 2, h, 2, g, kl))
        inv = np.zeros((h, 2, g, kl, g, N))
        for c in range(g):
            for p in range(h):
                k = slice(p * kl, (p + 1) * kl)
                fwd[c, :, 0, p, 0, c] = cos[:, k]
                fwd[c, :, 0, p, 1, c] = -sin[:, k]
                fwd[c, :, 1, p, 0, c] = -sin[:, k]
                fwd[c, :, 1, p, 1, c] = -cos[:, k]
                inv[p, 0, c, :, c] = cos[:, k].T
                inv[p, 1, c, :, c] = -sin[:, k].T
        self.z_fwd = bf(fwd.reshape(g * N, 2 * L))
        self.z_inv = bf(inv.reshape(L, g * N))
        self.y_fwd = bf(np.concatenate([cos.T, sin.T], 1))
        self.y_inv = bf(np.concatenate([cos, sin], 1))
        dup = lambda a: np.repeat(a, 2, axis=0)
        self.x_fwd = f32(np.concatenate([dup(cos.T), dup(sin.T)], 0) * scale)
        self.x_inv = f32(np.concatenate([dup(cos.T).T, dup(sin.T).T], 1) * scale)
        fold = np.zeros((G, 2, g, kl, 2, 128))
        unfold = np.zeros((128, G, 2, g, kl))
        for a in range(G):
            for c in range(g):
                for r in range(2):
                    fold[a, r, c, :, r, a * g + c] = 1
                    unfold[a * g + c, a, r, c, :] = 1
        self.fold = bf(fold.reshape(G * 128, 256))
        self.unfold = bf(unfold.reshape(128, G * 128))
        e1 = np.zeros((128, C, C))
        e2 = np.zeros((128, C, C))
        for c in range(C):
            e1[c, c, :] = 1
            e2[c, :, c] = 1
        self.e1 = bf(e1.reshape(128, C * C))
        self.e2 = bf(e2.reshape(128, C * C))
        self.e1t = bf(e1.reshape(128, C * C).T)
        self.e2t = bf(e2.reshape(128, C * C).T)
        spread = np.zeros((C, T16, 128))
        for c in range(C):
            spread[c, :, c] = 1
        self.spread = bf(spread.reshape(C * T16, 128))


def dot(a, b, precision=None):
    return jnp.dot(a, b, preferred_element_type=F32, precision=precision)


def dot_t(a, b):
    return lax.dot_general(a, b, (((1,), (1,)), ((), ())), preferred_element_type=F32)


def params(**more):
    return pltpu.CompilerParams(vmem_limit_bytes=LIMIT, **more)


def lines_of(plan, plane, x, z_fwd, y_fwd, out):
    for a in range(plan.G):
        wide = jnp.concatenate([plane(a * plan.g + c) for c in range(plan.g)], axis=1)
        section = dot(wide, z_fwd[...]).astype(BF)
        both = jnp.concatenate([section[:, : plan.L], section[:, plan.L :]], axis=0)
        line = dot(y_fwd[...], both)
        for p in range(plan.h):
            out[:, p, a * plan.X + x, :] = line[:, p * 128 : (p + 1) * 128]


def field_of(plan, lines, x, y_inv, z_inv, out):
    lane = lax.broadcasted_iota(jnp.int32, (M, 128), 1)
    sign = jnp.where(lane < 64, -1.0, 1.0).astype(F32)
    for a in range(plan.G):
        parts = []
        for p in range(plan.h):
            q = lines[:, p, a * plan.X + x, :]
            turned = pltpu.roll(q, 64, 1) * sign
            parts.append(jnp.concatenate([q, turned], axis=0))
        both = jnp.concatenate(parts, axis=1).astype(BF)
        across = dot(y_inv[...], both).astype(BF)
        values = dot(across, z_inv[...])
        for c in range(plan.g):
            out[a * plan.g + c] = values[:, c * plan.N : (c + 1) * plan.N]


def first_kernel(plan, field, z_fwd, y_fwd, out):
    x = pl.program_id(0)

    @pl.when(x == 0)
    def _():
        out[:, :, plan.rows :, :] = jnp.zeros((M, plan.h, 8, 128), F32)

    lines_of(plan, lambda c: field[c, 0], x, z_fwd, y_fwd, out)


def spread_weight(plan, weight, spread):
    rows = plan.C * T16
    half = dot(spread[...], weight[...]).astype(BF)
    full = dot_t(half, spread[...])
    r = lax.broadcasted_iota(jnp.int32, (rows, rows), 0) % T16
    c = lax.broadcasted_iota(jnp.int32, (rows, rows), 1) % T16
    return jnp.where(r == c, full, 0.0)


def slope_of(pre, cot):
    k = math.sqrt(2.0 / math.pi)
    square = pre * pre
    t = jnp.tanh(pre * (k + (k * 0.044715) * square))
    inner = pre * (0.5 * k + (1.5 * k * 0.044715) * square)
    return cot * (0.5 + 0.5 * t + inner * (1.0 - t * t))


def middle_kernel(plan, lines, field, cot, weight, bias, spread, y_inv, z_inv, z_fwd, y_fwd,
                  slope, out, pre, mix, acc, bias_acc):
    x = pl.program_id(0)
    C, N = plan.C, plan.N
    rows = C * T16

    @pl.when(x == 0)
    def _():
        out[:, :, plan.rows :, :] = jnp.zeros((M, plan.h, 8, 128), F32)
        mix[...] = spread_weight(plan, weight, spread).astype(BF)
        acc[...] = jnp.zeros_like(acc)
        bias_acc[...] = jnp.zeros_like(bias_acc)

    field_of(plan, lines, x, y_inv, z_inv, pre)

    def block(b, carry):
        ys = [pl.ds(pl.multiple_of(b * 2 * T16 + i * T16, T16), T16) for i in range(2)]
        wide = jnp.concatenate([field[:, 0, y, :].reshape(rows, N) for y in ys], axis=1)
        linear = dot(mix[...], wide)
        for i, y in enumerate(ys):
            part = linear[:, i * N : (i + 1) * N].reshape(C, T16, N)
            total = part + pre[:, y, :] + bias[...]
            got = slope_of(total, cot[:, 0, y, :].astype(F32)).astype(BF)
            slope[:, 0, y, :] = got
            wider = got.astype(F32)
            bias_acc[...] += wider[:, :8] + wider[:, 8:]
        return carry

    lax.fori_loop(0, N // (2 * T16), block, 0)
    lines_of(plan, lambda c: slope[c, 0], x, z_fwd, y_fwd, out)
    tall = lambda ref: jnp.concatenate(
        [ref[:, 0, i * T16 : (i + 1) * T16, :].reshape(rows, N) for i in range(N // T16)], axis=1
    )
    acc[...] += dot_t(tall(slope), tall(field))

    @pl.when(x == pl.num_programs(0) - 1)
    def _():
        r = lax.broadcasted_iota(jnp.int32, (rows, rows), 0) % T16
        c = lax.broadcasted_iota(jnp.int32, (rows, rows), 1) % T16
        kept = jnp.where(r == c, acc[...], 0.0)
        right = dot(kept, spread[...].astype(F32), HIGH)
        pointwise = jnp.sum(right.reshape(C, T16, 128), axis=1)
        ends = jnp.sum(jnp.sum(bias_acc[...], axis=1), axis=1, keepdims=True)
        lane = lax.broadcasted_iota(jnp.int32, (C, 128), 1)
        final = jnp.where(lane == C, ends, pointwise)
        for o in range(C):
            d, row = o // plan.rp, o % plan.rp
            out[d // plan.h, d % plan.h, plan.rows + row, :] = final[o]


def last_kernel(plan, lines, slope, weight, spread, y_inv, z_inv, grad, pre, mix):
    x = pl.program_id(0)
    C, N = plan.C, plan.N
    rows = C * T16

    @pl.when(x == 0)
    def _():
        mix[...] = spread_weight(plan, weight, spread).astype(BF)

    field_of(plan, lines, x, y_inv, z_inv, pre)

    def block(b, carry):
        ys = [pl.ds(pl.multiple_of(b * 2 * T16 + i * T16, T16), T16) for i in range(2)]
        wide = jnp.concatenate([slope[:, 0, y, :].reshape(rows, N) for y in ys], axis=1)
        linear = dot(mix[...], wide)
        for i, y in enumerate(ys):
            part = linear[:, i * N : (i + 1) * N].reshape(C, T16, N)
            grad[:, 0, y, :] = (part + pre[:, y, :]).astype(BF)
        return carry

    lax.fori_loop(0, N // (2 * T16), block, 0)


def whole(shape):
    return pl.BlockSpec(shape, lambda x: (0,) * len(shape))


def plane_spec(plan):
    return pl.BlockSpec((plan.C, 1, plan.N, plan.N), lambda x: (0, x, 0, 0))


def lines_shape(plan):
    return (M, plan.h, plan.rows_p, 128)


def run_first(plan, field):
    consts = [plan.z_fwd, plan.y_fwd]
    return pl.pallas_call(
        functools.partial(first_kernel, plan),
        grid=(plan.X,),
        in_specs=[plane_spec(plan)] + [whole(c.shape) for c in consts],
        out_specs=whole(lines_shape(plan)),
        out_shape=jax.ShapeDtypeStruct(lines_shape(plan), F32),
        compiler_params=params(),
        name="first",
    )(field, *[jnp.asarray(c) for c in consts])


def pad_weight(weight):
    return jnp.pad(weight, ((0, 128 - weight.shape[0]), (0, 128 - weight.shape[1])))


def run_middle(plan, lines, field, cot, weight, bias):
    rows = plan.C * T16
    consts = [plan.spread, plan.y_inv, plan.z_inv, plan.z_fwd, plan.y_fwd]
    wide = jnp.broadcast_to(bias[:, None, None], (plan.C, 1, 128))
    return pl.pallas_call(
        functools.partial(middle_kernel, plan),
        grid=(plan.X,),
        in_specs=[
            whole(lines_shape(plan)), plane_spec(plan), plane_spec(plan),
            whole((128, 128)), whole((plan.C, 1, 128)),
        ] + [whole(c.shape) for c in consts],
        out_specs=(plane_spec(plan), whole(lines_shape(plan))),
        out_shape=(
            jax.ShapeDtypeStruct(field.shape, BF),
            jax.ShapeDtypeStruct(lines_shape(plan), F32),
        ),
        scratch_shapes=[
            pltpu.VMEM((plan.C, plan.N, plan.N), F32),
            pltpu.VMEM((rows, rows), BF),
            pltpu.VMEM((rows, rows), F32),
            pltpu.VMEM((plan.C, 8, 128), F32),
        ],
        compiler_params=params(),
        name="middle",
    )(lines, field, cot, pad_weight(weight), wide, *[jnp.asarray(c) for c in consts])


def run_last(plan, lines, slope, weight):
    rows = plan.C * T16
    consts = [plan.spread, plan.y_inv, plan.z_inv]
    return pl.pallas_call(
        functools.partial(last_kernel, plan),
        grid=(plan.X,),
        in_specs=[whole(lines_shape(plan)), plane_spec(plan), whole((128, 128))]
        + [whole(c.shape) for c in consts],
        out_specs=plane_spec(plan),
        out_shape=jax.ShapeDtypeStruct(slope.shape, BF),
        scratch_shapes=[
            pltpu.VMEM((plan.C, plan.N, plan.N), F32),
            pltpu.VMEM((rows, rows), BF),
        ],
        compiler_params=params(),
        name="last",
    )(lines, slope, pad_weight(weight.T), *[jnp.asarray(c) for c in consts])


def modes_of(plan, lines, x_fwd, fold):
    P_ = plan.kl
    lane = lax.broadcasted_iota(jnp.int32, (2 * M, 128), 1)
    sign = jnp.where(lane < 64, 1.0, -1.0).astype(F32)
    rows = lax.broadcasted_iota(jnp.int32, (P_, 2 * M, 128), 0)
    lanes = lax.broadcasted_iota(jnp.int32, (P_, 2 * M, 128), 2) % P_
    own = rows == lanes
    parts = []
    for a in range(plan.G):
        block = lines[:, a * plan.X : (a + 1) * plan.X, :].reshape(plan.N, 128)
        both = dot(x_fwd[...], block, HIGH)
        u = both[: 2 * M] + sign * pltpu.roll(both[2 * M :], 64, 1)
        picked = jnp.where(own, u[None], 0.0)
        parts.append(picked.reshape(P_ * 2 * M, 128).astype(BF))
    return dot(jnp.concatenate(parts, axis=1), fold[...])


def lines_back(plan, real, imag, back, x_inv, unfold, out):
    P_ = plan.kl
    shape = (P_, 2 * M, 128)
    lane = lax.broadcasted_iota(jnp.int32, shape, 2)
    own = lax.broadcasted_iota(jnp.int32, shape, 0) == lane % P_
    same = (lax.broadcasted_iota(jnp.int32, shape, 1) % 2) == lane // 64
    is_real = lane < 64
    if back:
        sign_a, sign_b = jnp.where(is_real, 1.0, -1.0), 1.0
    else:
        sign_a, sign_b = 1.0, jnp.where(is_real, -1.0, 1.0)
    half = lax.broadcasted_iota(jnp.int32, (2 * M, 128), 1)
    turn = jnp.where(half < 64, -1.0, 1.0).astype(F32)
    for a in range(plan.G):
        cut = unfold[:, a * 128 : (a + 1) * 128]
        ra = dot(real, cut).reshape(shape) * sign_a
        rb = dot(imag, cut).reshape(shape) * sign_b
        v = jnp.sum(jnp.where(own, jnp.where(same, ra, rb), 0.0), axis=0)
        both = jnp.concatenate([v, turn * pltpu.roll(v, 64, 1)], axis=0)
        q = dot(x_inv[...], both, HIGH)
        out[:, a * plan.X : (a + 1) * plan.X, :] = q.reshape(plan.S, plan.X, 128)


def mix_forward(plan, lines, weight, x_fwd, x_inv, fold, unfold, e1, e2t, out, modes, ab):
    modes[...] = modes_of(plan, lines, x_fwd, fold).astype(BF)

    def chunk(b, carry):
        rows = pl.ds(pl.multiple_of(b * 64, 64), 64)
        w = weight[rows, :].astype(F32)
        for part in range(2):
            wide = dot(modes[rows, part * 128 : (part + 1) * 128], e1[...])
            ab[part, rows, :] = dot((wide * w).astype(BF), e2t[...]).astype(BF)
        return carry

    lax.fori_loop(0, modes.shape[0] // 64, chunk, 0)
    lines_back(plan, ab[0], ab[1], False, x_inv, unfold, out)
    out[:, plan.rows :, :] = jnp.zeros((plan.S, 8, 128), F32)


def mix_backward(plan, lines, weight, modes, x_fwd, x_inv, fold, unfold, e1, e2, e1t,
                 out, grad, held, turned, ab):
    s = modes_of(plan, lines, x_fwd, fold)
    held[...] = s.astype(BF)
    even = lax.broadcasted_iota(jnp.int32, (s.shape[0], 128), 0) % 2 == 0
    sr, si = s[:, :128], s[:, 128:]
    turned[:, :128] = jnp.where(even, sr, si).astype(BF)
    turned[:, 128:] = jnp.where(even, si, -sr).astype(BF)

    def chunk(b, carry):
        rows = pl.ds(pl.multiple_of(b * 64, 64), 64)
        w = weight[rows, :].astype(F32)
        for part in range(2):
            wide = dot(held[rows, part * 128 : (part + 1) * 128], e2[...])
            ab[part, rows, :] = dot((wide * w).astype(BF), e1t[...]).astype(BF)
        ur = dot(modes[rows, :128], e1[...])
        first = ur * dot(turned[rows, :128], e2[...])
        ui = dot(modes[rows, 128:], e1[...])
        grad[rows, :] = first + ui * dot(turned[rows, 128:], e2[...])
        return carry

    lax.fori_loop(0, s.shape[0] // 64, chunk, 0)
    lines_back(plan, ab[0], ab[1], True, x_inv, unfold, out)
    total = jnp.sum(lines[:, plan.rows :, :], axis=0) * float(plan.N) ** -1.5
    out[:, plan.rows :, :] = jnp.broadcast_to(total[None], (plan.S, 8, 128))


def run_mix_forward(plan, lines, weight):
    rows = plan.kl * 2 * M
    consts = [plan.x_fwd, plan.x_inv, plan.fold, plan.unfold, plan.e1, plan.e2t]
    return pl.pallas_call(
        functools.partial(mix_forward, plan),
        out_shape=(
            jax.ShapeDtypeStruct((plan.S, plan.rows_p, 128), F32),
            jax.ShapeDtypeStruct((rows, 256), BF),
        ),
        scratch_shapes=[pltpu.VMEM((2, rows, 128), BF)],
        compiler_params=params(),
        name="mix_forward",
    )(lines, weight, *[jnp.asarray(c) for c in consts])


def run_mix_backward(plan, lines, weight, modes):
    rows = plan.kl * 2 * M
    consts = [plan.x_fwd, plan.x_inv, plan.fold, plan.unfold, plan.e1, plan.e2, plan.e1t]
    return pl.pallas_call(
        functools.partial(mix_backward, plan),
        out_shape=(
            jax.ShapeDtypeStruct((plan.S, plan.rows_p, 128), F32),
            jax.ShapeDtypeStruct((rows, plan.pairs), F32),
        ),
        scratch_shapes=[
            pltpu.VMEM((rows, 256), BF),
            pltpu.VMEM((rows, 256), BF),
            pltpu.VMEM((2, rows, 128), BF),
        ],
        compiler_params=params(),
        name="mix_backward",
    )(lines, weight, modes, *[jnp.asarray(c) for c in consts])


def exchange_kernel(n, src, dst, send, recv, own):
    me = lax.axis_index("space")
    barrier = pltpu.get_barrier_semaphore()
    for k in range(1, n):
        pl.semaphore_signal(barrier, inc=1, device_id={"space": lax.rem(me + k, n)},
                            device_id_type=pl.DeviceIdType.MESH)
    pl.semaphore_wait(barrier, n - 1)
    copies = []
    for k in range(1, n):
        to = lax.rem(me + k, n)
        copy = pltpu.make_async_remote_copy(
            src_ref=src.at[to], dst_ref=dst.at[me], send_sem=send.at[k], recv_sem=recv.at[k],
            device_id={"space": to}, device_id_type=pl.DeviceIdType.MESH,
        )
        copy.start()
        copies.append(copy)
    local = pltpu.make_async_copy(src.at[me], dst.at[me], own)
    local.start()
    local.wait()
    for copy in copies:
        copy.wait()


def exchange(plan, blocks):
    n = plan.S
    return pl.pallas_call(
        functools.partial(exchange_kernel, n),
        out_shape=jax.ShapeDtypeStruct(blocks.shape, blocks.dtype),
        in_specs=[pl.BlockSpec(memory_space=pl.ANY)],
        out_specs=pl.BlockSpec(memory_space=pl.ANY),
        scratch_shapes=[
            pltpu.SemaphoreType.DMA((n,)),
            pltpu.SemaphoreType.DMA((n,)),
            pltpu.SemaphoreType.DMA,
        ],
        compiler_params=pltpu.CompilerParams(collective_id=0, has_side_effects=True),
        name="exchange",
    )(blocks)


def per_device(plan, inputs, cotangent, spectral_weight, pointwise_weight, bias):
    C = plan.C
    owners = (plan.S, plan.rows_p, 128)
    weight = spectral_weight.reshape(plan.kl * 2 * M, plan.pairs)
    lines = run_first(plan, inputs)
    got = exchange(plan, lines.reshape(owners))
    back, modes = run_mix_forward(plan, got, weight)
    got = exchange(plan, back).reshape(lines_shape(plan))
    slope, lines = run_middle(plan, got, inputs, cotangent, pointwise_weight, bias)
    got = exchange(plan, lines.reshape(owners))
    back, grad = run_mix_backward(plan, got, weight, modes)
    got = exchange(plan, back)
    grad_input = run_last(plan, got.reshape(lines_shape(plan)), slope, pointwise_weight)
    small = got[:, plan.rows : plan.rows + plan.rp, :].reshape(plan.S * plan.rp, 128)[:C]
    return (
        grad_input,
        grad.reshape(plan.kl, M, 2, plan.pairs),
        small[:, :C],
        small[:, C],
    )


def solution(mesh):
    space = mesh.shape["space"]

    def run(inputs, cotangent, spectral_weight, pointwise_weight, bias):
        channels = pointwise_weight.shape[0]
        plan = Plan(space, channels, inputs.shape[2])
        return jax.shard_map(
            functools.partial(per_device, plan),
            mesh=mesh,
            in_specs=(
                P("grp", "space", None, None),
                P("grp", "space", None, None),
                P("space", None, None, None),
                P(),
                P(),
            ),
            out_specs=(
                P("grp", "space", None, None),
                P(("grp", "space"), None, None, None),
                P("grp", None),
                P("grp"),
            ),
            check_vma=False,
        )(inputs, cotangent, spectral_weight, pointwise_weight, bias)

    return run
```

```python
import functools
import math

import jax
import jax.numpy as jnp
import numpy as np
from jax import lax
from jax.experimental import pallas as pl
from jax.experimental.pallas import tpu as pltpu
from jax.sharding import PartitionSpec as P

M = 16
T16 = 16
HIGH = lax.Precision.HIGHEST
BF = jnp.bfloat16
F32 = jnp.float32
LIMIT = 56 * 1024 * 1024


class Plan:
    def __init__(self, space, channels, width):
        self.S = space
        self.C = channels
        self.N = width
        self.X = width // space
        self.h = space // M
        self.kl = M // self.h
        self.g = 4 * self.h
        self.G = channels // self.g
        self.L = 128 * self.h
        self.rows = self.X * self.G
        self.rp = -(-channels // space)
        self.rows_p = self.rows + 8
        self.pairs = channels * channels
        self.tables()

    def tables(self):
        S, C, N, h, kl, g, G, L = self.S, self.C, self.N, self.h, self.kl, self.g, self.G, self.L
        ang = 2.0 * np.pi * ((np.arange(N)[:, None] * np.arange(M)[None, :]) % N) / N
        cos, sin = np.cos(ang), np.sin(ang)
        scale = float(N) ** -1.5
        bf = lambda a: np.asarray(a, np.float32).astype(jnp.bfloat16)
        f32 = lambda a: np.asarray(a, np.float32)
        fwd = np.zeros((g, N, 2, h, 2, g, kl))
        inv = np.zeros((h, 2, g, kl, g, N))
        for c in range(g):
            for p in range(h):
                k = slice(p * kl, (p + 1) * kl)
                fwd[c, :, 0, p, 0, c] = cos[:, k]
                fwd[c, :, 0, p, 1, c] = -sin[:, k]
                fwd[c, :, 1, p, 0, c] = -sin[:, k]
                fwd[c, :, 1, p, 1, c] = -cos[:, k]
                inv[p, 0, c, :, c] = cos[:, k].T
                inv[p, 1, c, :, c] = -sin[:, k].T
        self.z_fwd = bf(fwd.reshape(g * N, 2 * L))
        self.z_inv = bf(inv.reshape(L, g * N))
        self.y_fwd = bf(np.concatenate([cos.T, sin.T], 1))
        self.y_inv = bf(np.concatenate([cos, sin], 1))
        dup = lambda a: np.repeat(a, 2, axis=0)
        self.x_fwd = f32(np.concatenate([dup(cos.T), dup(sin.T)], 0) * scale)
        self.x_inv = f32(np.concatenate([dup(cos.T).T, dup(sin.T).T], 1) * scale)
        fold = np.zeros((G, 2, g, kl, 2, 128))
        unfold = np.zeros((128, G, 2, g, kl))
        for a in range(G):
            for c in range(g):
                for r in range(2):
                    fold[a, r, c, :, r, a * g + c] = 1
                    unfold[a * g + c, a, r, c, :] = 1
        self.fold = bf(fold.reshape(G * 128, 256))
        self.unfold = bf(unfold.reshape(128, G * 128))
        e1 = np.zeros((128, C, C))
        e2 = np.zeros((128, C, C))
        for c in range(C):
            e1[c, c, :] = 1
            e2[c, :, c] = 1
        self.e1 = bf(e1.reshape(128, C * C))
        self.e2 = bf(e2.reshape(128, C * C))
        self.e1t = bf(e1.reshape(128, C * C).T)
        self.e2t = bf(e2.reshape(128, C * C).T)
        spread = np.zeros((C, T16, 128))
        for c in range(C):
            spread[c, :, c] = 1
        self.spread = bf(spread.reshape(C * T16, 128))


def dot(a, b, precision=None):
    return jnp.dot(a, b, preferred_element_type=F32, precision=precision)


def dot_t(a, b):
    return lax.dot_general(a, b, (((1,), (1,)), ((), ())), preferred_element_type=F32)


def params(**more):
    return pltpu.CompilerParams(vmem_limit_bytes=LIMIT, **more)


def lines_of(plan, plane, x, z_fwd, y_fwd, out):
    size = plan.G // 3
    for start in range(0, plan.G, size):
        wide = jnp.concatenate(
            [
                jnp.concatenate([plane(a * plan.g + c) for c in range(plan.g)], axis=1)
                for a in range(start, start + size)
            ],
            axis=0,
        )
        section = dot(wide, z_fwd[...]).astype(BF)
        both = jnp.concatenate(
            [
                jnp.concatenate(
                    [section[i * plan.N : (i + 1) * plan.N, r * plan.L : (r + 1) * plan.L]
                     for i in range(size)],
                    axis=1,
                )
                for r in range(2)
            ],
            axis=0,
        )
        line = dot(y_fwd[...], both)
        for i in range(size):
            for p in range(plan.h):
                at = i * plan.L + p * 128
                out[:, p, (start + i) * plan.X + x, :] = line[:, at : at + 128]


def field_of(plan, lines, x, y_inv, z_inv, out):
    lane = lax.broadcasted_iota(jnp.int32, (M, 128), 1)
    sign = jnp.where(lane < 64, -1.0, 1.0).astype(F32)
    size = plan.G // 3
    for start in range(0, plan.G, size):
        parts = []
        for i in range(size):
            for p in range(plan.h):
                q = lines[:, p, (start + i) * plan.X + x, :]
                turned = pltpu.roll(q, 64, 1) * sign
                parts.append(jnp.concatenate([q, turned], axis=0))
        both = jnp.concatenate(parts, axis=1).astype(BF)
        across = dot(y_inv[...], both).astype(BF)
        tall = jnp.concatenate(
            [across[:, i * plan.L : (i + 1) * plan.L] for i in range(size)], axis=0
        )
        values = dot(tall, z_inv[...])
        for i in range(size):
            for c in range(plan.g):
                out[(start + i) * plan.g + c] = values[
                    i * plan.N : (i + 1) * plan.N, c * plan.N : (c + 1) * plan.N
                ]


def first_kernel(plan, field, z_fwd, y_fwd, out):
    x = pl.program_id(0)
    lines_of(plan, lambda c: field[c, 0], x, z_fwd, y_fwd, out)


def spread_weight(plan, weight, spread, transposed):
    rows = plan.C * T16
    narrow = spread[...][:, : plan.C]
    half = (dot_t if transposed else dot)(narrow, weight[...]).astype(BF)
    full = dot_t(half, narrow)
    r = lax.broadcasted_iota(jnp.int32, (rows, rows), 0) % T16
    c = lax.broadcasted_iota(jnp.int32, (rows, rows), 1) % T16
    return jnp.where(r == c, full, 0.0)


def slope_of(pre, cot):
    k = math.sqrt(2.0 / math.pi)
    square = pre * pre
    t = jnp.tanh(pre * (k + (k * 0.044715) * square))
    inner = pre * (0.5 * k + (1.5 * k * 0.044715) * square)
    return cot * (0.5 + 0.5 * t + inner * (1.0 - t * t))


def middle_kernel(plan, lines, field, cot, weight, bias, spread, y_inv, z_inv, z_fwd, y_fwd,
                  slope, out, pre, mix, acc, bias_acc):
    x = pl.program_id(0)
    C, N = plan.C, plan.N
    rows = C * T16

    @pl.when(x == 0)
    def _():
        out[:, :, plan.rows :, :] = jnp.zeros((M, plan.h, 8, 128), F32)
        mix[...] = spread_weight(plan, weight, spread, False).astype(BF)
        acc[...] = jnp.zeros_like(acc)
        bias_acc[...] = jnp.zeros_like(bias_acc)

    field_of(plan, lines, x, y_inv, z_inv, pre)

    def block(b, carry):
        ys = [pl.ds(pl.multiple_of(b * 2 * T16 + i * T16, T16), T16) for i in range(2)]
        wide = jnp.concatenate([field[:, 0, y, :].reshape(rows, N) for y in ys], axis=1)
        linear = dot(mix[...], wide)
        for i, y in enumerate(ys):
            part = linear[:, i * N : (i + 1) * N].reshape(C, T16, N)
            total = part + pre[:, y, :] + bias[...]
            got = slope_of(total, cot[:, 0, y, :].astype(F32)).astype(BF)
            slope[:, 0, y, :] = got
            wider = got.astype(F32)
            bias_acc[...] += wider[:, :8] + wider[:, 8:]
        return carry

    lax.fori_loop(0, N // (2 * T16), block, 0)
    lines_of(plan, lambda c: slope[c, 0], x, z_fwd, y_fwd, out)
    tall = lambda ref: jnp.concatenate(
        [ref[:, 0, i * T16 : (i + 1) * T16, :].reshape(rows, N) for i in range(N // T16)], axis=1
    )
    acc[...] += dot_t(tall(slope), tall(field))

    @pl.when(x == pl.num_programs(0) - 1)
    def _():
        r = lax.broadcasted_iota(jnp.int32, (rows, rows), 0) % T16
        c = lax.broadcasted_iota(jnp.int32, (rows, rows), 1) % T16
        kept = jnp.where(r == c, acc[...], 0.0)
        right = dot(kept, spread[...].astype(F32), HIGH)
        pointwise = jnp.sum(right.reshape(C, T16, 128), axis=1)
        ends = jnp.sum(jnp.sum(bias_acc[...], axis=1), axis=1, keepdims=True)
        lane = lax.broadcasted_iota(jnp.int32, (C, 128), 1)
        final = jnp.where(lane == C, ends, pointwise)
        for o in range(C):
            d, row = o // plan.rp, o % plan.rp
            out[d // plan.h, d % plan.h, plan.rows + row, :] = final[o]


def last_kernel(plan, lines, slope, weight, spread, y_inv, z_inv, grad, pre, mix):
    x = pl.program_id(0)
    C, N = plan.C, plan.N
    rows = C * T16

    @pl.when(x == 0)
    def _():
        mix[...] = spread_weight(plan, weight, spread, True).astype(BF)

    field_of(plan, lines, x, y_inv, z_inv, pre)

    def block(b, carry):
        ys = [pl.ds(pl.multiple_of(b * 2 * T16 + i * T16, T16), T16) for i in range(2)]
        wide = jnp.concatenate([slope[:, 0, y, :].reshape(rows, N) for y in ys], axis=1)
        linear = dot(mix[...], wide)
        for i, y in enumerate(ys):
            part = linear[:, i * N : (i + 1) * N].reshape(C, T16, N)
            grad[:, 0, y, :] = (part + pre[:, y, :]).astype(BF)
        return carry

    lax.fori_loop(0, N // (2 * T16), block, 0)


def whole(shape):
    return pl.BlockSpec(shape, lambda x: (0,) * len(shape))


def plane_spec(plan):
    return pl.BlockSpec((plan.C, 1, plan.N, plan.N), lambda x: (0, x, 0, 0))


def lines_shape(plan, spare=True):
    return (M, plan.h, plan.rows_p if spare else plan.rows, 128)


def run_first(plan, field):
    consts = [plan.z_fwd, plan.y_fwd]
    return pl.pallas_call(
        functools.partial(first_kernel, plan),
        grid=(plan.X,),
        in_specs=[plane_spec(plan)] + [whole(c.shape) for c in consts],
        out_specs=whole(lines_shape(plan, False)),
        out_shape=jax.ShapeDtypeStruct(lines_shape(plan, False), F32),
        compiler_params=params(),
        name="first",
    )(field, *[jnp.asarray(c) for c in consts])


def run_middle(plan, lines, field, cot, weight, bias):
    rows = plan.C * T16
    consts = [plan.spread, plan.y_inv, plan.z_inv, plan.z_fwd, plan.y_fwd]
    wide = jnp.broadcast_to(bias[:, None, None], (plan.C, 1, 128))
    return pl.pallas_call(
        functools.partial(middle_kernel, plan),
        grid=(plan.X,),
        in_specs=[
            whole(lines_shape(plan, False)), plane_spec(plan), plane_spec(plan),
            whole(weight.shape), whole((plan.C, 1, 128)),
        ] + [whole(c.shape) for c in consts],
        out_specs=(plane_spec(plan), whole(lines_shape(plan))),
        out_shape=(
            jax.ShapeDtypeStruct(field.shape, BF),
            jax.ShapeDtypeStruct(lines_shape(plan), F32),
        ),
        scratch_shapes=[
            pltpu.VMEM((plan.C, plan.N, plan.N), F32),
            pltpu.VMEM((rows, rows), BF),
            pltpu.VMEM((rows, rows), F32),
            pltpu.VMEM((plan.C, 8, 128), F32),
        ],
        compiler_params=params(),
        name="middle",
    )(lines, field, cot, weight, wide, *[jnp.asarray(c) for c in consts])


def run_last(plan, lines, slope, weight):
    rows = plan.C * T16
    consts = [plan.spread, plan.y_inv, plan.z_inv]
    return pl.pallas_call(
        functools.partial(last_kernel, plan),
        grid=(plan.X,),
        in_specs=[whole(lines_shape(plan)), plane_spec(plan), whole(weight.shape)]
        + [whole(c.shape) for c in consts],
        out_specs=plane_spec(plan),
        out_shape=jax.ShapeDtypeStruct(slope.shape, BF),
        scratch_shapes=[
            pltpu.VMEM((plan.C, plan.N, plan.N), F32),
            pltpu.VMEM((rows, rows), BF),
        ],
        compiler_params=params(),
        name="last",
    )(lines, slope, weight, *[jnp.asarray(c) for c in consts])


def modes_of(plan, lines, x_fwd, fold):
    P_ = plan.kl
    lane = lax.broadcasted_iota(jnp.int32, (2 * M, 128), 1)
    sign = jnp.where(lane < 64, 1.0, -1.0).astype(F32)
    rows = lax.broadcasted_iota(jnp.int32, (P_, 2 * M, 128), 0)
    lanes = lax.broadcasted_iota(jnp.int32, (P_, 2 * M, 128), 2) % P_
    own = rows == lanes
    parts = []
    for a in range(plan.G):
        block = lines[:, a * plan.X : (a + 1) * plan.X, :].reshape(plan.N, 128)
        both = dot(x_fwd[...], block, HIGH)
        u = both[: 2 * M] + sign * pltpu.roll(both[2 * M :], 64, 1)
        picked = jnp.where(own, u[None], 0.0)
        parts.append(picked.reshape(P_ * 2 * M, 128).astype(BF))
    return dot(jnp.concatenate(parts, axis=1), fold[...])


def lines_back(plan, real, imag, back, x_inv, unfold, out):
    P_ = plan.kl
    shape = (P_, 2 * M, 128)
    lane = lax.broadcasted_iota(jnp.int32, shape, 2)
    own = lax.broadcasted_iota(jnp.int32, shape, 0) == lane % P_
    same = (lax.broadcasted_iota(jnp.int32, shape, 1) % 2) == lane // 64
    is_real = lane < 64
    if back:
        sign_a, sign_b = jnp.where(is_real, 1.0, -1.0), 1.0
    else:
        sign_a, sign_b = 1.0, jnp.where(is_real, -1.0, 1.0)
    half = lax.broadcasted_iota(jnp.int32, (2 * M, 128), 1)
    turn = jnp.where(half < 64, -1.0, 1.0).astype(F32)
    for a in range(plan.G):
        cut = unfold[:, a * 128 : (a + 1) * 128]
        ra = dot(real, cut).reshape(shape) * sign_a
        rb = dot(imag, cut).reshape(shape) * sign_b
        v = jnp.sum(jnp.where(own, jnp.where(same, ra, rb), 0.0), axis=0)
        both = jnp.concatenate([v, turn * pltpu.roll(v, 64, 1)], axis=0)
        q = dot(x_inv[...], both, HIGH)
        out[:, a * plan.X : (a + 1) * plan.X, :] = q.reshape(plan.S, plan.X, 128)


def mix_forward(plan, lines, weight, x_fwd, x_inv, fold, unfold, e1, e2t, out, modes, ab):
    modes[...] = modes_of(plan, lines, x_fwd, fold).astype(BF)

    def chunk(b, carry):
        rows = pl.ds(pl.multiple_of(b * 64, 64), 64)
        w = weight[rows, :].astype(F32)
        for part in range(2):
            wide = dot(modes[rows, part * 128 : (part + 1) * 128], e1[...])
            ab[part, rows, :] = dot((wide * w).astype(BF), e2t[...]).astype(BF)
        return carry

    lax.fori_loop(0, modes.shape[0] // 64, chunk, 0)
    lines_back(plan, ab[0], ab[1], False, x_inv, unfold, out)


def mix_backward(plan, lines, weight, modes, x_fwd, x_inv, fold, unfold, e1, e2, e1t,
                 out, grad, held, turned, ab):
    s = modes_of(plan, lines, x_fwd, fold)
    held[...] = s.astype(BF)
    even = lax.broadcasted_iota(jnp.int32, (s.shape[0], 128), 0) % 2 == 0
    sr, si = s[:, :128], s[:, 128:]
    turned[:, :128] = jnp.where(even, sr, si).astype(BF)
    turned[:, 128:] = jnp.where(even, si, -sr).astype(BF)

    def chunk(b, carry):
        rows = pl.ds(pl.multiple_of(b * 64, 64), 64)
        w = weight[rows, :].astype(F32)
        for part in range(2):
            wide = dot(held[rows, part * 128 : (part + 1) * 128], e2[...])
            ab[part, rows, :] = dot((wide * w).astype(BF), e1t[...]).astype(BF)
        ur = dot(modes[rows, :128], e1[...])
        first = ur * dot(turned[rows, :128], e2[...])
        ui = dot(modes[rows, 128:], e1[...])
        grad[rows, :] = first + ui * dot(turned[rows, 128:], e2[...])
        return carry

    lax.fori_loop(0, s.shape[0] // 64, chunk, 0)
    lines_back(plan, ab[0], ab[1], True, x_inv, unfold, out)
    total = jnp.sum(lines[:, plan.rows :, :], axis=0) * float(plan.N) ** -1.5
    out[:, plan.rows :, :] = jnp.broadcast_to(total[None], (plan.S, 8, 128))


def run_mix_forward(plan, lines, weight):
    rows = plan.kl * 2 * M
    consts = [plan.x_fwd, plan.x_inv, plan.fold, plan.unfold, plan.e1, plan.e2t]
    return pl.pallas_call(
        functools.partial(mix_forward, plan),
        out_shape=(
            jax.ShapeDtypeStruct((plan.S, plan.rows, 128), F32),
            jax.ShapeDtypeStruct((rows, 256), BF),
        ),
        scratch_shapes=[pltpu.VMEM((2, rows, 128), BF)],
        compiler_params=params(),
        name="mix_forward",
    )(lines, weight, *[jnp.asarray(c) for c in consts])


def run_mix_backward(plan, lines, weight, modes):
    rows = plan.kl * 2 * M
    consts = [plan.x_fwd, plan.x_inv, plan.fold, plan.unfold, plan.e1, plan.e2, plan.e1t]
    return pl.pallas_call(
        functools.partial(mix_backward, plan),
        out_shape=(
            jax.ShapeDtypeStruct((plan.S, plan.rows_p, 128), F32),
            jax.ShapeDtypeStruct((rows, plan.pairs), F32),
        ),
        scratch_shapes=[
            pltpu.VMEM((rows, 256), BF),
            pltpu.VMEM((rows, 256), BF),
            pltpu.VMEM((2, rows, 128), BF),
        ],
        compiler_params=params(),
        name="mix_backward",
    )(lines, weight, modes, *[jnp.asarray(c) for c in consts])


def exchange_kernel(n, src, dst, send, recv, own):
    me = lax.axis_index("space")
    barrier = pltpu.get_barrier_semaphore()
    for k in range(1, n):
        pl.semaphore_signal(barrier, inc=1, device_id={"space": lax.rem(me + k, n)},
                            device_id_type=pl.DeviceIdType.MESH)
    pl.semaphore_wait(barrier, n - 1)
    copies = []
    for k in range(1, n):
        to = lax.rem(me + k, n)
        copy = pltpu.make_async_remote_copy(
            src_ref=src.at[to], dst_ref=dst.at[me], send_sem=send.at[k], recv_sem=recv.at[k],
            device_id={"space": to}, device_id_type=pl.DeviceIdType.MESH,
        )
        copy.start()
        copies.append(copy)
    local = pltpu.make_async_copy(src.at[me], dst.at[me], own)
    local.start()
    local.wait()
    for copy in copies:
        copy.wait()


def exchange(plan, blocks, call):
    n = plan.S
    return pl.pallas_call(
        functools.partial(exchange_kernel, n),
        out_shape=jax.ShapeDtypeStruct(blocks.shape, blocks.dtype),
        in_specs=[pl.BlockSpec(memory_space=pl.ANY)],
        out_specs=pl.BlockSpec(memory_space=pl.ANY),
        scratch_shapes=[
            pltpu.SemaphoreType.DMA((n,)),
            pltpu.SemaphoreType.DMA((n,)),
            pltpu.SemaphoreType.DMA,
        ],
        compiler_params=pltpu.CompilerParams(collective_id=call, has_side_effects=True),
        name="exchange" + str(call),
    )(blocks)


def per_device(plan, inputs, cotangent, spectral_weight, pointwise_weight, bias):
    C = plan.C
    owners = (plan.S, plan.rows_p, 128)
    weight = spectral_weight.reshape(plan.kl * 2 * M, plan.pairs)
    lines = run_first(plan, inputs)
    got = exchange(plan, lines.reshape(plan.S, plan.rows, 128), 0)
    back, modes = run_mix_forward(plan, got, weight)
    got = exchange(plan, back, 0).reshape(lines_shape(plan, False))
    slope, lines = run_middle(plan, got, inputs, cotangent, pointwise_weight, bias)
    got = exchange(plan, lines.reshape(owners), 1)
    back, grad = run_mix_backward(plan, got, weight, modes)
    got = exchange(plan, back, 1)
    grad_input = run_last(plan, got.reshape(lines_shape(plan)), slope, pointwise_weight)
    small = got[:, plan.rows : plan.rows + plan.rp, :].reshape(plan.S * plan.rp, 128)[:C]
    return (
        grad_input,
        grad.reshape(plan.kl, M, 2, plan.pairs),
        small[:, :C],
        small[:, C],
    )


def solution(mesh):
    space = mesh.shape["space"]

    def run(inputs, cotangent, spectral_weight, pointwise_weight, bias):
        channels = pointwise_weight.shape[0]
        plan = Plan(space, channels, inputs.shape[2])
        return jax.shard_map(
            functools.partial(per_device, plan),
            mesh=mesh,
            in_specs=(
                P("grp", "space", None, None),
                P("grp", "space", None, None),
                P("space", None, None, None),
                P(),
                P(),
            ),
            out_specs=(
                P("grp", "space", None, None),
                P(("grp", "space"), None, None, None),
                P("grp", None),
                P("grp"),
            ),
            check_vma=False,
        )(inputs, cotangent, spectral_weight, pointwise_weight, bias)

    return run
```

```python
import functools
import math

import jax
import jax.numpy as jnp
import numpy as np
from jax import lax
from jax.experimental import pallas as pl
from jax.experimental.pallas import tpu as pltpu
from jax.sharding import PartitionSpec as P

M = 16
T16 = 16
HIGH = lax.Precision.HIGHEST
BF = jnp.bfloat16
F32 = jnp.float32
LIMIT = 56 * 1024 * 1024


class Plan:
    def __init__(self, space, channels, width):
        self.S = space
        self.C = channels
        self.N = width
        self.X = width // space
        self.h = space // M
        self.kl = M // self.h
        self.g = 4 * self.h
        self.G = channels // self.g
        self.L = 128 * self.h
        self.rows = self.X * self.G
        self.rp = -(-channels // space)
        self.rows_p = self.rows + 8
        self.pairs = channels * channels
        self.tables()

    def tables(self):
        S, C, N, h, kl, g, G, L = self.S, self.C, self.N, self.h, self.kl, self.g, self.G, self.L
        ang = 2.0 * np.pi * ((np.arange(N)[:, None] * np.arange(M)[None, :]) % N) / N
        cos, sin = np.cos(ang), np.sin(ang)
        scale = float(N) ** -1.5
        bf = lambda a: np.asarray(a, np.float32).astype(jnp.bfloat16)
        f32 = lambda a: np.asarray(a, np.float32)
        fwd = np.zeros((g, N, 2, h, 2, g, kl))
        inv = np.zeros((h, 2, g, kl, g, N))
        for c in range(g):
            for p in range(h):
                k = slice(p * kl, (p + 1) * kl)
                fwd[c, :, 0, p, 0, c] = cos[:, k]
                fwd[c, :, 0, p, 1, c] = -sin[:, k]
                fwd[c, :, 1, p, 0, c] = -sin[:, k]
                fwd[c, :, 1, p, 1, c] = -cos[:, k]
                inv[p, 0, c, :, c] = cos[:, k].T
                inv[p, 1, c, :, c] = -sin[:, k].T
        self.z_fwd = bf(fwd.reshape(g * N, 2 * L))
        self.z_inv = bf(inv.reshape(L, g * N))
        self.y_fwd = bf(np.concatenate([cos.T, sin.T], 1))
        self.y_inv = bf(np.concatenate([cos, sin], 1))
        dup = lambda a: np.repeat(a, 2, axis=0)
        self.x_fwd = f32(np.concatenate([dup(cos.T), dup(sin.T)], 0) * scale)
        self.x_inv = f32(np.concatenate([dup(cos.T).T, dup(sin.T).T], 1) * scale)
        fold = np.zeros((G, 2, g, kl, 2, 128))
        unfold = np.zeros((128, G, 2, g, kl))
        for a in range(G):
            for c in range(g):
                for r in range(2):
                    fold[a, r, c, :, r, a * g + c] = 1
                    unfold[a * g + c, a, r, c, :] = 1
        self.fold = bf(fold.reshape(G * 128, 256))
        self.unfold = bf(unfold.reshape(128, G * 128))
        e1 = np.zeros((128, C, C))
        e2 = np.zeros((128, C, C))
        for c in range(C):
            e1[c, c, :] = 1
            e2[c, :, c] = 1
        self.e1 = bf(e1.reshape(128, C * C))
        self.e2 = bf(e2.reshape(128, C * C))
        self.e1t = bf(e1.reshape(128, C * C).T)
        self.e2t = bf(e2.reshape(128, C * C).T)
        spread = np.zeros((C, T16, 128))
        for c in range(C):
            spread[c, :, c] = 1
        self.spread = bf(spread.reshape(C * T16, 128))


def dot(a, b, precision=None):
    return jnp.dot(a, b, preferred_element_type=F32, precision=precision)


def dot_t(a, b):
    return lax.dot_general(a, b, (((1,), (1,)), ((), ())), preferred_element_type=F32)


def params(**more):
    return pltpu.CompilerParams(vmem_limit_bytes=LIMIT, **more)


def lines_of(plan, plane, x, z_fwd, y_fwd, out):
    size = plan.G // 3
    for start in range(0, plan.G, size):
        wide = jnp.concatenate(
            [
                jnp.concatenate([plane(a * plan.g + c) for c in range(plan.g)], axis=1)
                for a in range(start, start + size)
            ],
            axis=0,
        )
        section = dot(wide, z_fwd[...]).astype(BF)
        both = jnp.concatenate(
            [
                jnp.concatenate(
                    [section[i * plan.N : (i + 1) * plan.N, r * plan.L : (r + 1) * plan.L]
                     for i in range(size)],
                    axis=1,
                )
                for r in range(2)
            ],
            axis=0,
        )
        line = dot(y_fwd[...], both)
        for i in range(size):
            for p in range(plan.h):
                at = i * plan.L + p * 128
                out[:, p, (start + i) * plan.X + x, :] = line[:, at : at + 128]


def field_of(plan, lines, x, y_inv, z_inv, out):
    lane = lax.broadcasted_iota(jnp.int32, (M, 128), 1)
    sign = jnp.where(lane < 64, -1.0, 1.0).astype(F32)
    size = plan.G // 3
    for start in range(0, plan.G, size):
        parts = []
        for i in range(size):
            for p in range(plan.h):
                q = lines[:, p, (start + i) * plan.X + x, :]
                turned = pltpu.roll(q, 64, 1) * sign
                parts.append(jnp.concatenate([q, turned], axis=0))
        both = jnp.concatenate(parts, axis=1).astype(BF)
        across = dot(y_inv[...], both).astype(BF)
        tall = jnp.concatenate(
            [across[:, i * plan.L : (i + 1) * plan.L] for i in range(size)], axis=0
        )
        values = dot(tall, z_inv[...])
        for i in range(size):
            for c in range(plan.g):
                out[(start + i) * plan.g + c] = values[
                    i * plan.N : (i + 1) * plan.N, c * plan.N : (c + 1) * plan.N
                ]


def first_kernel(plan, field, z_fwd, y_fwd, out):
    x = pl.program_id(0)
    lines_of(plan, lambda c: field[c, 0], x, z_fwd, y_fwd, out)


def spread_weight(plan, weight, spread, transposed):
    rows = plan.C * T16
    narrow = spread[...][:, : plan.C]
    half = (dot_t if transposed else dot)(narrow, weight[...]).astype(BF)
    full = dot_t(half, narrow)
    r = lax.broadcasted_iota(jnp.int32, (rows, rows), 0) % T16
    c = lax.broadcasted_iota(jnp.int32, (rows, rows), 1) % T16
    return jnp.where(r == c, full, 0.0)


def slope_of(pre, cot):
    k = math.sqrt(2.0 / math.pi)
    square = pre * pre
    t = jnp.tanh(pre * (k + (k * 0.044715) * square))
    inner = pre * (0.5 * k + (1.5 * k * 0.044715) * square)
    return cot * (0.5 + 0.5 * t + inner * (1.0 - t * t))


def middle_kernel(plan, lines, field, cot, weight, bias, spread, y_inv, z_inv, z_fwd, y_fwd,
                  slope, out, pre, mix, acc, bias_acc):
    x = pl.program_id(0)
    C, N = plan.C, plan.N
    rows = C * T16

    @pl.when(x == 0)
    def _():
        out[:, :, plan.rows :, :] = jnp.zeros((M, plan.h, 8, 128), F32)
        mix[...] = spread_weight(plan, weight, spread, False).astype(BF)
        acc[...] = jnp.zeros_like(acc)
        bias_acc[...] = jnp.zeros_like(bias_acc)

    field_of(plan, lines, x, y_inv, z_inv, pre)

    def block(b, carry):
        ys = [pl.ds(pl.multiple_of(b * 2 * T16 + i * T16, T16), T16) for i in range(2)]
        wide = jnp.concatenate([field[:, 0, y, :].reshape(rows, N) for y in ys], axis=1)
        linear = dot(mix[...], wide)
        for i, y in enumerate(ys):
            part = linear[:, i * N : (i + 1) * N].reshape(C, T16, N)
            total = part + pre[:, y, :] + bias[...]
            got = slope_of(total, cot[:, 0, y, :].astype(F32)).astype(BF)
            slope[:, 0, y, :] = got
            wider = got.astype(F32)
            bias_acc[...] += wider[:, :8] + wider[:, 8:]
        return carry

    lax.fori_loop(0, N // (2 * T16), block, 0, unroll=True)
    lines_of(plan, lambda c: slope[c, 0], x, z_fwd, y_fwd, out)
    tall = lambda ref: jnp.concatenate(
        [ref[:, 0, i * T16 : (i + 1) * T16, :].reshape(rows, N) for i in range(N // T16)], axis=1
    )
    acc[...] += dot_t(tall(slope), tall(field))

    @pl.when(x == pl.num_programs(0) - 1)
    def _():
        r = lax.broadcasted_iota(jnp.int32, (rows, rows), 0) % T16
        c = lax.broadcasted_iota(jnp.int32, (rows, rows), 1) % T16
        kept = jnp.where(r == c, acc[...], 0.0)
        right = dot(kept, spread[...].astype(F32), HIGH)
        pointwise = jnp.sum(right.reshape(C, T16, 128), axis=1)
        ends = jnp.sum(jnp.sum(bias_acc[...], axis=1), axis=1, keepdims=True)
        lane = lax.broadcasted_iota(jnp.int32, (C, 128), 1)
        final = jnp.where(lane == C, ends, pointwise)
        for o in range(C):
            d, row = o // plan.rp, o % plan.rp
            out[d // plan.h, d % plan.h, plan.rows + row, :] = final[o]


def last_kernel(plan, lines, slope, weight, spread, y_inv, z_inv, grad, pre, mix):
    x = pl.program_id(0)
    C, N = plan.C, plan.N
    rows = C * T16

    @pl.when(x == 0)
    def _():
        mix[...] = spread_weight(plan, weight, spread, True).astype(BF)

    field_of(plan, lines, x, y_inv, z_inv, pre)

    def block(b, carry):
        ys = [pl.ds(pl.multiple_of(b * 2 * T16 + i * T16, T16), T16) for i in range(2)]
        wide = jnp.concatenate([slope[:, 0, y, :].reshape(rows, N) for y in ys], axis=1)
        linear = dot(mix[...], wide)
        for i, y in enumerate(ys):
            part = linear[:, i * N : (i + 1) * N].reshape(C, T16, N)
            grad[:, 0, y, :] = (part + pre[:, y, :]).astype(BF)
        return carry

    lax.fori_loop(0, N // (2 * T16), block, 0, unroll=True)


def whole(shape):
    return pl.BlockSpec(shape, lambda x: (0,) * len(shape))


def plane_spec(plan):
    return pl.BlockSpec((plan.C, 1, plan.N, plan.N), lambda x: (0, x, 0, 0))


def lines_shape(plan, spare=True):
    return (M, plan.h, plan.rows_p if spare else plan.rows, 128)


def run_first(plan, field):
    consts = [plan.z_fwd, plan.y_fwd]
    return pl.pallas_call(
        functools.partial(first_kernel, plan),
        grid=(plan.X,),
        in_specs=[plane_spec(plan)] + [whole(c.shape) for c in consts],
        out_specs=whole(lines_shape(plan, False)),
        out_shape=jax.ShapeDtypeStruct(lines_shape(plan, False), F32),
        compiler_params=params(),
        name="first",
    )(field, *[jnp.asarray(c) for c in consts])


def run_middle(plan, lines, field, cot, weight, bias):
    rows = plan.C * T16
    consts = [plan.spread, plan.y_inv, plan.z_inv, plan.z_fwd, plan.y_fwd]
    wide = jnp.broadcast_to(bias[:, None, None], (plan.C, 1, 128))
    return pl.pallas_call(
        functools.partial(middle_kernel, plan),
        grid=(plan.X,),
        in_specs=[
            whole(lines_shape(plan, False)), plane_spec(plan), plane_spec(plan),
            whole(weight.shape), whole((plan.C, 1, 128)),
        ] + [whole(c.shape) for c in consts],
        out_specs=(plane_spec(plan), whole(lines_shape(plan))),
        out_shape=(
            jax.ShapeDtypeStruct(field.shape, BF),
            jax.ShapeDtypeStruct(lines_shape(plan), F32),
        ),
        scratch_shapes=[
            pltpu.VMEM((plan.C, plan.N, plan.N), F32),
            pltpu.VMEM((rows, rows), BF),
            pltpu.VMEM((rows, rows), F32),
            pltpu.VMEM((plan.C, 8, 128), F32),
        ],
        compiler_params=params(),
        name="middle",
    )(lines, field, cot, weight, wide, *[jnp.asarray(c) for c in consts])


def run_last(plan, lines, slope, weight):
    rows = plan.C * T16
    consts = [plan.spread, plan.y_inv, plan.z_inv]
    return pl.pallas_call(
        functools.partial(last_kernel, plan),
        grid=(plan.X,),
        in_specs=[whole(lines_shape(plan)), plane_spec(plan), whole(weight.shape)]
        + [whole(c.shape) for c in consts],
        out_specs=plane_spec(plan),
        out_shape=jax.ShapeDtypeStruct(slope.shape, BF),
        scratch_shapes=[
            pltpu.VMEM((plan.C, plan.N, plan.N), F32),
            pltpu.VMEM((rows, rows), BF),
        ],
        compiler_params=params(),
        name="last",
    )(lines, slope, weight, *[jnp.asarray(c) for c in consts])


def modes_of(plan, lines, x_fwd, fold):
    P_ = plan.kl
    lane = lax.broadcasted_iota(jnp.int32, (2 * M, 128), 1)
    sign = jnp.where(lane < 64, 1.0, -1.0).astype(F32)
    rows = lax.broadcasted_iota(jnp.int32, (P_, 2 * M, 128), 0)
    lanes = lax.broadcasted_iota(jnp.int32, (P_, 2 * M, 128), 2) % P_
    own = rows == lanes
    parts = []
    for a in range(plan.G):
        block = lines[:, a * plan.X : (a + 1) * plan.X, :].reshape(plan.N, 128)
        both = dot(x_fwd[...], block, HIGH)
        u = both[: 2 * M] + sign * pltpu.roll(both[2 * M :], 64, 1)
        picked = jnp.where(own, u[None], 0.0)
        parts.append(picked.reshape(P_ * 2 * M, 128).astype(BF))
    return dot(jnp.concatenate(parts, axis=1), fold[...])


def lines_back(plan, real, imag, back, x_inv, unfold, out):
    P_ = plan.kl
    shape = (P_, 2 * M, 128)
    lane = lax.broadcasted_iota(jnp.int32, shape, 2)
    own = lax.broadcasted_iota(jnp.int32, shape, 0) == lane % P_
    same = (lax.broadcasted_iota(jnp.int32, shape, 1) % 2) == lane // 64
    is_real = lane < 64
    if back:
        sign_a, sign_b = jnp.where(is_real, 1.0, -1.0), 1.0
    else:
        sign_a, sign_b = 1.0, jnp.where(is_real, -1.0, 1.0)
    half = lax.broadcasted_iota(jnp.int32, (2 * M, 128), 1)
    turn = jnp.where(half < 64, -1.0, 1.0).astype(F32)
    for a in range(plan.G):
        cut = unfold[:, a * 128 : (a + 1) * 128]
        ra = dot(real, cut).reshape(shape) * sign_a
        rb = dot(imag, cut).reshape(shape) * sign_b
        v = jnp.sum(jnp.where(own, jnp.where(same, ra, rb), 0.0), axis=0)
        both = jnp.concatenate([v, turn * pltpu.roll(v, 64, 1)], axis=0)
        q = dot(x_inv[...], both, HIGH)
        out[:, a * plan.X : (a + 1) * plan.X, :] = q.reshape(plan.S, plan.X, 128)


def mix_forward(plan, lines, weight, x_fwd, x_inv, fold, unfold, e1, e2t, out, modes, ab):
    modes[...] = modes_of(plan, lines, x_fwd, fold).astype(BF)

    def chunk(b, carry):
        rows = pl.ds(pl.multiple_of(b * 64, 64), 64)
        w = weight[rows, :].astype(F32)
        for part in range(2):
            wide = dot(modes[rows, part * 128 : (part + 1) * 128], e1[...])
            ab[part, rows, :] = dot((wide * w).astype(BF), e2t[...]).astype(BF)
        return carry

    lax.fori_loop(0, modes.shape[0] // 64, chunk, 0, unroll=2)
    lines_back(plan, ab[0], ab[1], False, x_inv, unfold, out)


def mix_backward(plan, lines, weight, modes, x_fwd, x_inv, fold, unfold, e1, e2, e1t,
                 out, grad, held, turned, ab):
    s = modes_of(plan, lines, x_fwd, fold)
    held[...] = s.astype(BF)
    even = lax.broadcasted_iota(jnp.int32, (s.shape[0], 128), 0) % 2 == 0
    sr, si = s[:, :128], s[:, 128:]
    turned[:, :128] = jnp.where(even, sr, si).astype(BF)
    turned[:, 128:] = jnp.where(even, si, -sr).astype(BF)

    def chunk(b, carry):
        rows = pl.ds(pl.multiple_of(b * 64, 64), 64)
        w = weight[rows, :].astype(F32)
        for part in range(2):
            wide = dot(held[rows, part * 128 : (part + 1) * 128], e2[...])
            ab[part, rows, :] = dot((wide * w).astype(BF), e1t[...]).astype(BF)
        ur = dot(modes[rows, :128], e1[...])
        first = ur * dot(turned[rows, :128], e2[...])
        ui = dot(modes[rows, 128:], e1[...])
        grad[rows, :] = first + ui * dot(turned[rows, 128:], e2[...])
        return carry

    lax.fori_loop(0, s.shape[0] // 64, chunk, 0, unroll=2)
    lines_back(plan, ab[0], ab[1], True, x_inv, unfold, out)
    total = jnp.sum(lines[:, plan.rows :, :], axis=0) * float(plan.N) ** -1.5
    out[:, plan.rows :, :] = jnp.broadcast_to(total[None], (plan.S, 8, 128))


def run_mix_forward(plan, lines, weight):
    rows = plan.kl * 2 * M
    consts = [plan.x_fwd, plan.x_inv, plan.fold, plan.unfold, plan.e1, plan.e2t]
    return pl.pallas_call(
        functools.partial(mix_forward, plan),
        out_shape=(
            jax.ShapeDtypeStruct((plan.S, plan.rows, 128), F32),
            jax.ShapeDtypeStruct((rows, 256), BF),
        ),
        scratch_shapes=[pltpu.VMEM((2, rows, 128), BF)],
        compiler_params=params(),
        name="mix_forward",
    )(lines, weight, *[jnp.asarray(c) for c in consts])


def run_mix_backward(plan, lines, weight, modes):
    rows = plan.kl * 2 * M
    consts = [plan.x_fwd, plan.x_inv, plan.fold, plan.unfold, plan.e1, plan.e2, plan.e1t]
    return pl.pallas_call(
        functools.partial(mix_backward, plan),
        out_shape=(
            jax.ShapeDtypeStruct((plan.S, plan.rows_p, 128), F32),
            jax.ShapeDtypeStruct((rows, plan.pairs), F32),
        ),
        scratch_shapes=[
            pltpu.VMEM((rows, 256), BF),
            pltpu.VMEM((rows, 256), BF),
            pltpu.VMEM((2, rows, 128), BF),
        ],
        compiler_params=params(),
        name="mix_backward",
    )(lines, weight, modes, *[jnp.asarray(c) for c in consts])


def exchange_kernel(n, src, dst, send, recv, own):
    me = lax.axis_index("space")
    barrier = pltpu.get_barrier_semaphore()
    for k in range(1, n):
        pl.semaphore_signal(barrier, inc=1, device_id={"space": lax.rem(me + k, n)},
                            device_id_type=pl.DeviceIdType.MESH)
    pl.semaphore_wait(barrier, n - 1)
    copies = []
    for k in range(1, n):
        to = lax.rem(me + k, n)
        copy = pltpu.make_async_remote_copy(
            src_ref=src.at[to], dst_ref=dst.at[me], send_sem=send.at[k], recv_sem=recv.at[k],
            device_id={"space": to}, device_id_type=pl.DeviceIdType.MESH,
        )
        copy.start()
        copies.append(copy)
    local = pltpu.make_async_copy(src.at[me], dst.at[me], own)
    local.start()
    local.wait()
    for copy in copies:
        copy.wait()


def exchange(plan, blocks, call):
    n = plan.S
    return pl.pallas_call(
        functools.partial(exchange_kernel, n),
        out_shape=jax.ShapeDtypeStruct(blocks.shape, blocks.dtype),
        in_specs=[pl.BlockSpec(memory_space=pl.ANY)],
        out_specs=pl.BlockSpec(memory_space=pl.ANY),
        scratch_shapes=[
            pltpu.SemaphoreType.DMA((n,)),
            pltpu.SemaphoreType.DMA((n,)),
            pltpu.SemaphoreType.DMA,
        ],
        compiler_params=pltpu.CompilerParams(collective_id=call, has_side_effects=True),
        name="exchange" + str(call),
    )(blocks)


def per_device(plan, inputs, cotangent, spectral_weight, pointwise_weight, bias):
    C = plan.C
    owners = (plan.S, plan.rows_p, 128)
    weight = spectral_weight.reshape(plan.kl * 2 * M, plan.pairs)
    lines = run_first(plan, inputs)
    got = exchange(plan, lines.reshape(plan.S, plan.rows, 128), 0)
    back, modes = run_mix_forward(plan, got, weight)
    got = exchange(plan, back, 0).reshape(lines_shape(plan, False))
    slope, lines = run_middle(plan, got, inputs, cotangent, pointwise_weight, bias)
    got = exchange(plan, lines.reshape(owners), 1)
    back, grad = run_mix_backward(plan, got, weight, modes)
    got = exchange(plan, back, 1)
    grad_input = run_last(plan, got.reshape(lines_shape(plan)), slope, pointwise_weight)
    small = got[:, plan.rows : plan.rows + plan.rp, :].reshape(plan.S * plan.rp, 128)[:C]
    return (
        grad_input,
        grad.reshape(plan.kl, M, 2, plan.pairs),
        small[:, :C],
        small[:, C],
    )


def solution(mesh):
    space = mesh.shape["space"]

    def run(inputs, cotangent, spectral_weight, pointwise_weight, bias):
        channels = pointwise_weight.shape[0]
        plan = Plan(space, channels, inputs.shape[2])
        return jax.shard_map(
            functools.partial(per_device, plan),
            mesh=mesh,
            in_specs=(
                P("grp", "space", None, None),
                P("grp", "space", None, None),
                P("space", None, None, None),
                P(),
                P(),
            ),
            out_specs=(
                P("grp", "space", None, None),
                P(("grp", "space"), None, None, None),
                P("grp", None),
                P("grp"),
            ),
            check_vma=False,
        )(inputs, cotangent, spectral_weight, pointwise_weight, bias)

    return run
```
